32 devices in a mesh: row: 8 (over y, x, core), col: 4 (over z).
Axes of the slice: x: 2, y: 2, z: 4, core: 2. Of those that a mesh axis runs over, the one named last changes fastest.
Arguments:
- mask: float32 [4096, 2048], P('row', 'col'), may hold values from -1 to 1
- row_taps: float32 [24, 65], replicated, may hold values from -0.75 to 0.75
- col_taps: float32 [24, 65], replicated, may hold values from -0.75 to 0.75
- kernel_weights: float32 [24], replicated, may hold values from 0.1 to 1
- target: float32 [4096, 2048], P('row', 'col'), may hold values from 0 to 1
- density: int32 [8, 4], P('row', 'col'), may hold values from 0 to 2
Outputs:
- resist: float32 [4096, 2048], P('row', 'col')
- gradient: float32 [4096, 2048], P('row', 'col')
The draws below stay inside these ranges and needn't reach their ends.
All inputs are finite; a program needn't handle non-finite values.
Results may differ from the reference program's by a relative error of at most 0.0003.
Values sent between devices are 32-bit elements; how exact they have to be, the bound alone decides.
A program may use at most 192 MiB of HBM per device.

```python
import math
import jax
import jax.numpy as jnp
from jax import lax

HR = 512
HC = 512
R = 32
NK = 24
BLOCK_ROWS = 8
BLOCK_COLS = 4
NR = 4096
NC = 2048


def with_ends(values, stream_key, smallest, high):
    index_at = [jax.random.randint(jax.random.fold_in(stream_key, axis), (), 0, length) for axis, length in enumerate(values.shape)]
    longest = values.shape.index(max(values.shape))
    neighbour = index_at[:longest] + [(index_at[longest] + 1) % values.shape[longest]] + index_at[longest + 1:]
    return values.at[tuple(index_at)].set(smallest).at[tuple(neighbour)].set(high)


def steps_of(own_key, dims, split, least, high):
    level, own = 1.0, jax.random.fold_in(own_key, 6)
    for position, parts in split:
        heights = jnp.exp(jax.random.uniform(jax.random.fold_in(own, position), (parts,), jnp.float32, least / len(split), high / len(split)))
        level = level * jnp.repeat(heights, dims[position] // parts).reshape([-1 if axis == position else 1 for axis in range(len(dims))])
    return level


def noise(key, shape, deviation, reach, kind=jnp.bfloat16):
    array = deviation * jax.random.normal(key, shape, jnp.float32)
    return jnp.clip(array, min=-reach, max=reach).astype(kind)


def setup_inputs(seed: int = 0) -> dict:
    key_of = jax.random.split(jax.random.key(seed), 7)
    return {
        "mask": jnp.clip(jax.random.uniform(key_of[0], (NR, NC), jnp.float32, -1.0, 1.0) * steps_of(key_of[0], (NR, NC), ((0, 8), (1, 4)), -0.4, 0.0), -1.0, 1.0),
        "row_taps": noise(key_of[1], (NK, 2 * R + 1), (2 * R + 1) ** -0.5, 0.75, jnp.float32),
        "col_taps": noise(key_of[2], (NK, 2 * R + 1), (2 * R + 1) ** -0.5, 0.75, jnp.float32),
        "kernel_weights": jnp.clip(jnp.exp(jax.random.uniform(key_of[3], (NK,), jnp.float32, math.log(0.1), math.log(1.0))), 0.1, 1.0),
        "target": jnp.clip(1.0 * jax.random.uniform(key_of[4], (NR, NC), jnp.float32) ** steps_of(key_of[4], (NR, NC), ((0, 8), (1, 4)), -0.2, 0.2), 0.0, 1.0),
        "density": with_ends(jax.random.randint(key_of[5], (BLOCK_ROWS, BLOCK_COLS), 0, 3), jax.random.fold_in(key_of[5], 1), 0, 2).astype(jnp.int32),
    }


def along_rows(field, taps):
    return lax.conv_general_dilated(field[None, None], taps[None, None, :, None], (1, 1), ((R, R), (0, 0)), precision=lax.Precision.HIGHEST)[0, 0]


def along_cols(field, taps):
    return lax.conv_general_dilated(field[None, None], taps[None, None, None, :], (1, 1), ((0, 0), (R, R)), precision=lax.Precision.HIGHEST)[0, 0]


def spread_tiles(values):
    return jnp.repeat(jnp.repeat(values, HR, axis=0), HC, axis=1)


def reference(mask, row_taps, col_taps, kernel_weights, target, density):
    counts = (NK // 3) * (density + 1)
    cell_counts = spread_tiles(counts)
    cumulative = jnp.cumsum(kernel_weights)
    weight_sum = spread_tiles(cumulative[counts - 1])
    order = jnp.arange(NK, dtype=jnp.int32)

    def forward(intensity, inputs):
        kernel, row_tap, col_tap, weight = inputs
        field = along_cols(along_rows(mask, row_tap), col_tap)
        return intensity + jnp.where(kernel < cell_counts, weight * field * field, 0.0), None

    intensity, unused = lax.scan(forward, jnp.zeros(mask.shape, jnp.float32), (order, row_taps, col_taps, kernel_weights))
    intensity = intensity / weight_sum
    resist = jax.nn.sigmoid(6.0 * (intensity - 0.33))
    error = (resist - target) * 6.0 * resist * (1.0 - resist)

    def backward(gradient, inputs):
        kernel, row_tap, col_tap, weight = inputs
        field = along_cols(along_rows(mask, row_tap), col_tap)
        field_grad = jnp.where(kernel < cell_counts, 2.0 * weight * error * field / weight_sum, 0.0)
        return gradient + along_cols(along_rows(field_grad, row_tap[::-1]), col_tap[::-1]), None

    gradient, unused = lax.scan(backward, jnp.zeros(mask.shape, jnp.float32), (order, row_taps, col_taps, kernel_weights))
    return resist, gradient
```

```python
import functools

import jax
import jax.numpy as jnp
from jax import lax
from jax.experimental import pallas as pl
from jax.experimental.pallas import tpu as pltpu
from jax.sharding import PartitionSpec as P

resist_slope = 6.0
resist_level = 0.33
f32, bf16 = jnp.float32, jnp.bfloat16

FB = 16
AB = 32
CHUNK = 128
WIN = 256


def split(x):
    hi = x.astype(bf16)
    return hi, (x - hi.astype(f32)).astype(bf16)


def split_outside(x):
    hi = lax.reduce_precision(x, 8, 7)
    return hi.astype(bf16), (x - hi).astype(bf16)


def mm(a, b):
    return lax.dot_general(a, b, (((1,), (0,)), ((), ())), preferred_element_type=f32)


def tile_kernel(nk, height, breadth, reach, scal_ref, mask_ref, target_ref, fwd_ref, adj_ref, cvec_ref, avec_ref,
                resist_ref, grad_ref,
                mhi, mlo, ahi, alo, field, bhi, blo, z, chi, clo, dhi, dlo, inten):
    out_win = WIN - 2 * reach
    nwin = -(-breadth // out_win)
    span = FB + 2 * reach
    aspan = AB + 2 * reach
    rows3 = nwin * CHUNK

    inv_sum = scal_ref[0]
    for w in range(nwin):
        m = mask_ref[:, w * out_win:w * out_win + WIN]
        hi, lo = split(m)
        mhi[w] = hi
        mlo[w] = lo
    z[...] = jnp.zeros_like(z)

    def tables(k, carry):
        row = jnp.broadcast_to(cvec_ref[pl.ds(k, 1), :], (WIN, WIN))
        hi, lo = split(pltpu.roll(row, 0, 1, stride=1, stride_axis=0))
        chi[k] = hi
        clo[k] = lo
        row = jnp.broadcast_to(avec_ref[pl.ds(k, 1), :], (WIN, WIN))
        hi, lo = split(pltpu.roll(row, 0, 1, stride=1, stride_axis=0))
        dhi[k] = hi
        dlo[k] = lo
        return carry

    lax.fori_loop(0, nk, tables, 0)

    lane = lax.broadcasted_iota(jnp.int32, (CHUNK, WIN), 1)

    def chunk(c, carry):
        base = pl.multiple_of(c * CHUNK, CHUNK)

        def rows_forward(b, carry):
            start = pl.multiple_of(base + b * FB, FB)
            to = pl.multiple_of(b * FB, FB)
            for w in range(nwin):
                xh = mhi[w, pl.ds(start, span), :]
                xl = mlo[w, pl.ds(start, span), :]
                x = jnp.concatenate([xh, xl, xh, jnp.zeros((256 - 3 * span, WIN), bf16)], axis=0)
                y = mm(fwd_ref[...], x)
                hi, lo = split(y)
                ahi[:, pl.ds(w * CHUNK + to, FB), :] = hi.reshape(nk, FB, WIN)
                alo[:, pl.ds(w * CHUNK + to, FB), :] = lo.reshape(nk, FB, WIN)
            return carry

        lax.fori_loop(0, CHUNK // FB, rows_forward, 0)
        inten[...] = jnp.zeros_like(inten)

        def cols_forward(k, carry):
            ah, al = ahi[k], alo[k]
            ch, cl = chi[k], clo[k]
            f = mm(jnp.concatenate([ah, al, ah], axis=1), jnp.concatenate([ch, ch, cl], axis=0))
            field[k] = f
            inten[...] += f * f
            return carry

        lax.fori_loop(0, nk, cols_forward, 0)

        t = target_ref[pl.ds(base, CHUNK), :]
        outs = []
        for w in range(nwin):
            width = min(out_win, breadth - w * out_win)
            tw = t[:, w * out_win:min(w * out_win + WIN, breadth)]
            if tw.shape[1] < WIN:
                tw = jnp.concatenate([tw, jnp.zeros((CHUNK, WIN - tw.shape[1]), f32)], axis=1)
            i = inten[w * CHUNK:(w + 1) * CHUNK, :] * inv_sum
            r = 1.0 / (1.0 + jnp.exp(-resist_slope * (i - resist_level)))
            e = (r - tw) * resist_slope * r * (1.0 - r) * (2.0 * inv_sum)
            inten[w * CHUNK:(w + 1) * CHUNK, :] = jnp.where(lane < width, e, 0.0)
            outs.append(r[:, :width])
        resist_ref[pl.ds(base, CHUNK), :] = jnp.concatenate(outs, axis=1)

        def cols_adjoint(k, carry):
            gh, gl = split(field[k] * inten[...])
            dh, dl = dhi[k], dlo[k]
            b = mm(jnp.concatenate([gh, gl, gh], axis=1), jnp.concatenate([dh, dh, dl], axis=0))
            hi, lo = split(b)
            to = pl.multiple_of(k * AB, AB)
            bhi[:, pl.ds(to, AB), :] = hi.reshape(rows3 // AB, AB, WIN)
            blo[:, pl.ds(to, AB), :] = lo.reshape(rows3 // AB, AB, WIN)
            return carry

        lax.fori_loop(0, nk, cols_adjoint, 0)

        def rows_adjoint(b, carry):
            start = pl.multiple_of(base + b * AB, AB)
            for w in range(nwin):
                at = w * (CHUNK // AB) + b
                p = mm(adj_ref[...], bhi[at])
                q = mm(adj_ref[:aspan, :], blo[at])
                z[w, pl.ds(start, aspan), :] += p[:aspan] + p[aspan:] + q
            return carry

        lax.fori_loop(0, CHUNK // AB, rows_adjoint, 0)
        return carry

    lax.fori_loop(0, height // CHUNK, chunk, 0)

    both = 2 * reach
    pieces = []
    for w in range(nwin):
        left = z[w, :, :both]
        if w:
            left = left + z[w - 1, :, out_win:]
        pieces.append(left)
        end = min(out_win, breadth + both - w * out_win)
        pieces.append(z[w, :, both:end])
    grad_ref[...] = jnp.concatenate(pieces, axis=1)


def shift_pairs(axis):
    count = lax.axis_size(axis)
    forward = [(i, i + 1) for i in range(count - 1)]
    return forward, [(b, a) for a, b in forward]


def padded(block, sides, width):
    for axis, dim in sides:
        forward, backward = shift_pairs(axis)
        size = block.shape[dim]
        low = lax.ppermute(lax.slice_in_dim(block, size - width, size, axis=dim), axis, forward)
        high = lax.ppermute(lax.slice_in_dim(block, 0, width, axis=dim), axis, backward)
        block = jnp.concatenate([low, block, high], axis=dim)
    return block


def folded(block, sides, width):
    for axis, dim in sides:
        forward, backward = shift_pairs(axis)
        size = block.shape[dim]
        low = lax.ppermute(lax.slice_in_dim(block, size - width, size, axis=dim), axis, forward)
        high = lax.ppermute(lax.slice_in_dim(block, 0, width, axis=dim), axis, backward)
        inner = lax.slice_in_dim(block, width, size - width, axis=dim)
        rest = size - 3 * width
        lows = [(0, 0, 0), (0, 0, 0)]
        highs = [(0, 0, 0), (0, 0, 0)]
        lows[dim] = (0, rest, 0)
        highs[dim] = (rest, 0, 0)
        block = inner + lax.pad(low, 0.0, lows) + lax.pad(high, 0.0, highs)
    return block


def toeplitz(taps, block):
    span = taps.shape[1]
    length = block + span - 1
    p = jnp.arange(span)[:, None, None]
    i = jnp.arange(block)[None, :, None]
    j = jnp.arange(length)[None, None, :]
    onehot = (j - i == p).astype(bf16)
    return jnp.einsum("kp,pij->kij", taps, onehot, preferred_element_type=f32).astype(bf16)


def shards(mask, row_taps, col_taps, kernel_weights, target, density):
    height, breadth = mask.shape
    nk, taps = row_taps.shape
    reach = (taps - 1) // 2
    count = (nk // 3) * (density[0, 0] + 1)
    active = jnp.arange(nk) < count
    inv_sum = 1.0 / jnp.sum(jnp.where(active, kernel_weights, 0.0))
    scale = jnp.where(active, jnp.sqrt(kernel_weights), 0.0)

    out_win = WIN - 2 * reach
    nwin = -(-breadth // out_win)
    need = (nwin - 1) * out_win + WIN
    ext = padded(mask, (("row", 0), ("col", 1)), reach)
    ext = jnp.pad(ext, ((0, 0), (0, need - ext.shape[1])))

    rhi, rlo = split_outside(row_taps * scale[:, None])
    both = jnp.concatenate([rhi, rlo], axis=0)
    fwd = toeplitz(both, FB).reshape(2, nk * FB, FB + 2 * reach)
    fwd = jnp.concatenate([fwd[0], fwd[0], fwd[1], jnp.zeros((nk * FB, 256 - 3 * fwd.shape[2]), bf16)], axis=1)
    adj = toeplitz(both, AB).reshape(2, nk, AB, AB + 2 * reach)
    adj = adj.transpose(0, 3, 1, 2).reshape(2 * (AB + 2 * reach), nk * AB)
    avec = jnp.pad(col_taps, ((0, 0), (0, WIN - taps)))
    cvec = jnp.concatenate([col_taps[:, :1], jnp.zeros((nk, WIN - taps), f32), col_taps[:, :0:-1]], axis=1)

    eh = height + 2 * reach
    rows3 = nwin * CHUNK
    vmem = pl.BlockSpec(memory_space=pltpu.VMEM)
    resist, grad = pl.pallas_call(
        functools.partial(tile_kernel, nk, height, breadth, reach),
        out_shape=(
            jax.ShapeDtypeStruct((height, breadth), f32),
            jax.ShapeDtypeStruct((eh, breadth + 2 * reach), f32),
        ),
        in_specs=[pl.BlockSpec(memory_space=pltpu.SMEM)] + [vmem] * 6,
        out_specs=(vmem, vmem),
        scratch_shapes=[
            pltpu.VMEM((nwin, eh, WIN), bf16),
            pltpu.VMEM((nwin, eh, WIN), bf16),
            pltpu.VMEM((nk, rows3, WIN), bf16),
            pltpu.VMEM((nk, rows3, WIN), bf16),
            pltpu.VMEM((nk, rows3, WIN), f32),
            pltpu.VMEM((rows3 // AB, nk * AB, WIN), bf16),
            pltpu.VMEM((rows3 // AB, nk * AB, WIN), bf16),
            pltpu.VMEM((nwin, eh, WIN), f32),
        ] + [pltpu.VMEM((nk, WIN, WIN), bf16)] * 4 + [pltpu.VMEM((rows3, WIN), f32)],
        compiler_params=pltpu.CompilerParams(vmem_limit_bytes=60 * 1024 * 1024),
    )(inv_sum[None], ext, target, fwd, adj, cvec, avec)
    gradient = folded(grad, (("col", 1), ("row", 0)), reach)
    return resist, gradient


def solution(mesh):
    return jax.shard_map(
        shards,
        mesh=mesh,
        in_specs=(P("row", "col"), P(), P(), P(), P("row", "col"), P("row", "col")),
        out_specs=(P("row", "col"), P("row", "col")),
        check_vma=False,
    )
```

```python
import functools

import jax
import jax.numpy as jnp
from jax import lax
from jax.experimental import pallas as pl
from jax.experimental.pallas import tpu as pltpu
from jax.sharding import PartitionSpec as P

resist_slope = 6.0
resist_level = 0.33
f32, bf16 = jnp.float32, jnp.bfloat16

FB = 16
AB = 32
CHUNK = 128
WIN = 256


def split(x):
    hi = x.astype(bf16)
    return hi, (x - hi.astype(f32)).astype(bf16)


def split_outside(x):
    hi = lax.reduce_precision(x, 8, 7)
    return hi.astype(bf16), (x - hi).astype(bf16)


def mm(a, b):
    return lax.dot_general(a, b, (((1,), (0,)), ((), ())), preferred_element_type=f32)


def tile_kernel(nk, height, breadth, reach, scal_ref, mask_ref, target_ref, fwd_ref, adj_ref, cvec_ref, avec_ref,
                resist_ref, grad_ref,
                mhi, mlo, ahi, alo, field, bhi, blo, z, chi, clo, dhi, dlo, inten):
    out_win = WIN - 2 * reach
    nwin = -(-breadth // out_win)
    span = FB + 2 * reach
    aspan = AB + 2 * reach
    rows3 = nwin * CHUNK

    inv_sum = scal_ref[0]
    for w in range(nwin):
        m = mask_ref[:, w * out_win:w * out_win + WIN]
        hi, lo = split(m)
        mhi[w] = hi
        mlo[w] = lo
    z[...] = jnp.zeros_like(z)

    def tables(k, carry):
        row = jnp.broadcast_to(cvec_ref[pl.ds(k, 1), :], (WIN, WIN))
        hi, lo = split(pltpu.roll(row, 0, 1, stride=1, stride_axis=0))
        chi[k] = hi
        clo[k] = lo
        row = jnp.broadcast_to(avec_ref[pl.ds(k, 1), :], (WIN, WIN))
        hi, lo = split(pltpu.roll(row, 0, 1, stride=1, stride_axis=0))
        dhi[k] = hi
        dlo[k] = lo
        return carry

    lax.fori_loop(0, nk, tables, 0)

    lane = lax.broadcasted_iota(jnp.int32, (CHUNK, WIN), 1)

    def chunk(c, carry):
        base = pl.multiple_of(c * CHUNK, CHUNK)

        def rows_forward(b, carry):
            start = pl.multiple_of(base + b * FB, FB)
            to = pl.multiple_of(b * FB, FB)
            for w in range(nwin):
                xh = mhi[w, pl.ds(start, span), :]
                xl = mlo[w, pl.ds(start, span), :]
                x = jnp.concatenate([xh, xl, xh, jnp.zeros((256 - 3 * span, WIN), bf16)], axis=0)
                y = mm(fwd_ref[...], x)
                hi, lo = split(y)
                ahi[:, pl.ds(w * CHUNK + to, FB), :] = hi.reshape(nk, FB, WIN)
                alo[:, pl.ds(w * CHUNK + to, FB), :] = lo.reshape(nk, FB, WIN)
            return carry

        lax.fori_loop(0, CHUNK // FB, rows_forward, 0)
        inten[...] = jnp.zeros_like(inten)

        def cols_forward(k, carry):
            ah, al = ahi[k], alo[k]
            ch, cl = chi[k], clo[k]
            f = mm(jnp.concatenate([ah, al, ah], axis=1), jnp.concatenate([ch, ch, cl], axis=0))
            field[k] = f
            inten[...] += f * f
            return carry

        lax.fori_loop(0, nk, cols_forward, 0)

        t = target_ref[pl.ds(base, CHUNK), :]
        outs = []
        for w in range(nwin):
            width = min(out_win, breadth - w * out_win)
            tw = t[:, w * out_win:min(w * out_win + WIN, breadth)]
            if tw.shape[1] < WIN:
                tw = jnp.concatenate([tw, jnp.zeros((CHUNK, WIN - tw.shape[1]), f32)], axis=1)
            i = inten[w * CHUNK:(w + 1) * CHUNK, :] * inv_sum
            r = 1.0 / (1.0 + jnp.exp(-resist_slope * (i - resist_level)))
            e = (r - tw) * resist_slope * r * (1.0 - r) * (2.0 * inv_sum)
            inten[w * CHUNK:(w + 1) * CHUNK, :] = jnp.where(lane < width, e, 0.0)
            outs.append(r[:, :width])
        resist_ref[pl.ds(base, CHUNK), :] = jnp.concatenate(outs, axis=1)

        def cols_adjoint(k, carry):
            gh, gl = split(field[k] * inten[...])
            dh, dl = dhi[k], dlo[k]
            b = mm(jnp.concatenate([gh, gl, gh], axis=1), jnp.concatenate([dh, dh, dl], axis=0))
            hi, lo = split(b)
            to = pl.multiple_of(k * AB, AB)
            bhi[:, pl.ds(to, AB), :] = hi.reshape(rows3 // AB, AB, WIN)
            blo[:, pl.ds(to, AB), :] = lo.reshape(rows3 // AB, AB, WIN)
            return carry

        lax.fori_loop(0, nk, cols_adjoint, 0)

        def rows_adjoint(b, carry):
            start = pl.multiple_of(base + b * AB, AB)
            for w in range(nwin):
                at = w * (CHUNK // AB) + b
                p = mm(adj_ref[...], bhi[at])
                q = mm(adj_ref[:aspan, :], blo[at])
                z[w, pl.ds(start, aspan), :] += p[:aspan] + p[aspan:] + q
            return carry

        lax.fori_loop(0, CHUNK // AB, rows_adjoint, 0)
        return carry

    lax.fori_loop(0, height // CHUNK, chunk, 0)

    both = 2 * reach
    pieces = []
    for w in range(nwin):
        left = z[w, :, :both]
        if w:
            left = left + z[w - 1, :, out_win:]
        pieces.append(left)
        end = min(out_win, breadth + both - w * out_win)
        pieces.append(z[w, :, both:end])
    grad_ref[...] = jnp.concatenate(pieces, axis=1)


def sides(axis):
    me, count = lax.axis_index(axis), lax.axis_size(axis)
    return ((axis, me - 1, me > 0), (axis, me + 1, me < count - 1))


def greet(neighbours):
    barrier = pltpu.get_barrier_semaphore()
    for axis, at, there in neighbours:
        @pl.when(there)
        def _():
            pl.semaphore_signal(barrier, inc=1, device_id={axis: at}, device_id_type=pl.DeviceIdType.MESH)
    pl.semaphore_wait(barrier, sum(there.astype(jnp.int32) for _, _, there in neighbours))


def exchange(neighbours, sources, landing, send_sem, recv_sem):
    def copy(i):
        axis, at, _ = neighbours[i]
        return pltpu.make_async_remote_copy(
            src_ref=sources[i], dst_ref=landing.at[1 - i], send_sem=send_sem.at[i], recv_sem=recv_sem.at[1 - i],
            device_id={axis: at}, device_id_type=pl.DeviceIdType.MESH)

    def incoming(i):
        axis, at, _ = neighbours[i]
        return pltpu.make_async_remote_copy(
            src_ref=sources[i], dst_ref=landing.at[i], send_sem=send_sem.at[i], recv_sem=recv_sem.at[i],
            device_id={axis: at}, device_id_type=pl.DeviceIdType.MESH)

    for i in range(2):
        @pl.when(neighbours[i][2])
        def _():
            copy(i).start()
    for i in range(2):
        @pl.when(neighbours[i][2])
        def _():
            incoming(i).wait_recv()

        @pl.when(jnp.logical_not(neighbours[i][2]))
        def _():
            landing[i] = jnp.zeros(landing.shape[1:], f32)
    for i in range(2):
        @pl.when(neighbours[i][2])
        def _():
            copy(i).wait_send()


def pack(strip):
    width = strip.shape[1]
    folds = 128 // width
    part = strip.shape[0] // folds
    return jnp.concatenate([strip[i * part:(i + 1) * part] for i in range(folds)], axis=1)


def unpack(packed, width):
    return jnp.concatenate([packed[:, i:i + width] for i in range(0, 128, width)], axis=0)


def widen_kernel(reach, mask_ref, ext_ref, rows, colsend, cols, sems):
    height, breadth = mask_ref.shape
    up_down, left_right = sides("row"), sides("col")
    greet(up_down + left_right)
    exchange(up_down, (mask_ref.at[pl.ds(0, reach)], mask_ref.at[pl.ds(height - reach, reach)]), rows, sems.at[0], sems.at[1])
    colsend[0] = pack(jnp.concatenate([rows[0, :, :reach], mask_ref[:, :reach], rows[1, :, :reach]], axis=0))
    colsend[1] = pack(jnp.concatenate(
        [rows[0, :, breadth - reach:], mask_ref[:, breadth - reach:], rows[1, :, breadth - reach:]], axis=0))
    exchange(left_right, (colsend.at[0], colsend.at[1]), cols, sems.at[2], sems.at[3])
    left, right = unpack(cols[0], reach), unpack(cols[1], reach)
    extra = ext_ref.shape[1] - breadth - 2 * reach
    for part, lo, hi in ((rows[0], 0, reach), (mask_ref[...], reach, reach + height),
                         (rows[1], reach + height, height + 2 * reach)):
        ext_ref[lo:hi, :] = jnp.concatenate(
            [left[lo:hi], part, right[lo:hi], jnp.zeros((hi - lo, extra), f32)], axis=1)


def fold_kernel(reach, g_ref, out_ref, colsend, cols, acc, rows, sems):
    height, breadth = out_ref.shape
    up_down, left_right = sides("row"), sides("col")
    greet(up_down + left_right)
    colsend[0] = pack(g_ref[:, :reach])
    colsend[1] = pack(g_ref[:, reach + breadth:])
    exchange(left_right, (colsend.at[0], colsend.at[1]), cols, sems.at[0], sems.at[1])
    left, right = unpack(cols[0], reach), unpack(cols[1], reach)
    acc[...] = jnp.concatenate(
        [g_ref[:, reach:2 * reach] + left, g_ref[:, 2 * reach:breadth], g_ref[:, breadth:breadth + reach] + right], axis=1)
    exchange(up_down, (acc.at[pl.ds(0, reach)], acc.at[pl.ds(height + reach, reach)]), rows, sems.at[2], sems.at[3])
    out_ref[:reach, :] = acc[reach:2 * reach, :] + rows[0]
    out_ref[reach:height - reach, :] = acc[2 * reach:height, :]
    out_ref[height - reach:, :] = acc[height:height + reach, :] + rows[1]


def strips(height, breadth, reach):
    packed = pltpu.VMEM((2, (height + 2 * reach) * reach // 128, 128), f32)
    return packed, pltpu.VMEM((2, reach, breadth), f32), pltpu.SemaphoreType.DMA((4, 2))


def widen(mask, reach, need):
    height, breadth = mask.shape
    packed, rows, sems = strips(height, breadth, reach)
    vmem = pl.BlockSpec(memory_space=pltpu.VMEM)
    return pl.pallas_call(
        functools.partial(widen_kernel, reach),
        out_shape=jax.ShapeDtypeStruct((height + 2 * reach, need), f32),
        in_specs=[vmem], out_specs=vmem,
        scratch_shapes=[rows, packed, packed, sems],
        compiler_params=pltpu.CompilerParams(
            collective_id=0, has_side_effects=True, vmem_limit_bytes=16 * 1024 * 1024),
    )(mask)


def fold(grad, reach):
    height, breadth = grad.shape[0] - 2 * reach, grad.shape[1] - 2 * reach
    packed, rows, sems = strips(height, breadth, reach)
    vmem = pl.BlockSpec(memory_space=pltpu.VMEM)
    return pl.pallas_call(
        functools.partial(fold_kernel, reach),
        out_shape=jax.ShapeDtypeStruct((height, breadth), f32),
        in_specs=[vmem], out_specs=vmem,
        scratch_shapes=[packed, packed, pltpu.VMEM((height + 2 * reach, breadth), f32), rows, sems],
        compiler_params=pltpu.CompilerParams(
            collective_id=1, has_side_effects=True, vmem_limit_bytes=16 * 1024 * 1024),
    )(grad)


def toeplitz(taps, block):
    span = taps.shape[1]
    length = block + span - 1
    p = jnp.arange(span)[:, None, None]
    i = jnp.arange(block)[None, :, None]
    j = jnp.arange(length)[None, None, :]
    onehot = (j - i == p).astype(bf16)
    return jnp.einsum("kp,pij->kij", taps, onehot, preferred_element_type=f32).astype(bf16)


def shards(mask, row_taps, col_taps, kernel_weights, target, density):
    height, breadth = mask.shape
    nk, taps = row_taps.shape
    reach = (taps - 1) // 2
    count = (nk // 3) * (density[0, 0] + 1)
    active = jnp.arange(nk) < count
    inv_sum = 1.0 / jnp.sum(jnp.where(active, kernel_weights, 0.0))
    scale = jnp.where(active, jnp.sqrt(kernel_weights), 0.0)

    out_win = WIN - 2 * reach
    nwin = -(-breadth // out_win)
    need = (nwin - 1) * out_win + WIN
    ext = widen(mask, reach, need)

    rhi, rlo = split_outside(row_taps * scale[:, None])
    both = jnp.concatenate([rhi, rlo], axis=0)
    fwd = toeplitz(both, FB).reshape(2, nk * FB, FB + 2 * reach)
    fwd = jnp.concatenate([fwd[0], fwd[0], fwd[1], jnp.zeros((nk * FB, 256 - 3 * fwd.shape[2]), bf16)], axis=1)
    adj = toeplitz(both, AB).reshape(2, nk, AB, AB + 2 * reach)
    adj = adj.transpose(0, 3, 1, 2).reshape(2 * (AB + 2 * reach), nk * AB)
    avec = jnp.pad(col_taps, ((0, 0), (0, WIN - taps)))
    cvec = jnp.concatenate([col_taps[:, :1], jnp.zeros((nk, WIN - taps), f32), col_taps[:, :0:-1]], axis=1)

    eh = height + 2 * reach
    rows3 = nwin * CHUNK
    vmem = pl.BlockSpec(memory_space=pltpu.VMEM)
    resist, grad = pl.pallas_call(
        functools.partial(tile_kernel, nk, height, breadth, reach),
        out_shape=(
            jax.ShapeDtypeStruct((height, breadth), f32),
            jax.ShapeDtypeStruct((eh, breadth + 2 * reach), f32),
        ),
        in_specs=[pl.BlockSpec(memory_space=pltpu.SMEM)] + [vmem] * 6,
        out_specs=(vmem, vmem),
        scratch_shapes=[
            pltpu.VMEM((nwin, eh, WIN), bf16),
            pltpu.VMEM((nwin, eh, WIN), bf16),
            pltpu.VMEM((nk, rows3, WIN), bf16),
            pltpu.VMEM((nk, rows3, WIN), bf16),
            pltpu.VMEM((nk, rows3, WIN), f32),
            pltpu.VMEM((rows3 // AB, nk * AB, WIN), bf16),
            pltpu.VMEM((rows3 // AB, nk * AB, WIN), bf16),
            pltpu.VMEM((nwin, eh, WIN), f32),
        ] + [pltpu.VMEM((nk, WIN, WIN), bf16)] * 4 + [pltpu.VMEM((rows3, WIN), f32)],
        compiler_params=pltpu.CompilerParams(vmem_limit_bytes=60 * 1024 * 1024),
    )(inv_sum[None], ext, target, fwd, adj, cvec, avec)
    gradient = fold(grad, reach)
    return resist, gradient


def solution(mesh):
    return jax.shard_map(
        shards,
        mesh=mesh,
        in_specs=(P("row", "col"), P(), P(), P(), P("row", "col"), P("row", "col")),
        out_specs=(P("row", "col"), P("row", "col")),
        check_vma=False,
    )
```

```python
import functools

import jax
import jax.numpy as jnp
from jax import lax
from jax.experimental import pallas as pl
from jax.experimental.pallas import tpu as pltpu
from jax.sharding import PartitionSpec as P

resist_slope = 6.0
resist_level = 0.33
f32, bf16 = jnp.float32, jnp.bfloat16

FB = 16
AB = 32
CHUNK = 128
WIN = 256


def split(x):
    hi = x.astype(bf16)
    return hi, (x - hi.astype(f32)).astype(bf16)


def split_outside(x):
    hi = lax.reduce_precision(x, 8, 7)
    return hi.astype(bf16), (x - hi).astype(bf16)


def mm(a, b):
    return lax.dot_general(a, b, (((1,), (0,)), ((), ())), preferred_element_type=f32)


def tile_kernel(nk, height, breadth, reach, scal_ref, mask_ref, target_ref, fwd_ref, adj_ref, cvec_ref, avec_ref,
                resist_ref, grad_ref,
                mhi, mlo, ahi, alo, field, bhi, blo, z, chi, clo, dhi, dlo, inten):
    out_win = WIN - 2 * reach
    nwin = -(-breadth // out_win)
    span = FB + 2 * reach
    aspan = AB + 2 * reach
    rows3 = nwin * CHUNK

    inv_sum = scal_ref[0]
    for w in range(nwin):
        m = mask_ref[:, w * out_win:w * out_win + WIN]
        hi, lo = split(m)
        mhi[w] = hi
        mlo[w] = lo
    z[...] = jnp.zeros_like(z)

    def tables(k, carry):
        row = jnp.broadcast_to(cvec_ref[pl.ds(k, 1), :], (WIN, WIN))
        hi, lo = split(pltpu.roll(row, 0, 1, stride=1, stride_axis=0))
        chi[k] = hi
        clo[k] = lo
        row = jnp.broadcast_to(avec_ref[pl.ds(k, 1), :], (WIN, WIN))
        hi, lo = split(pltpu.roll(row, 0, 1, stride=1, stride_axis=0))
        dhi[k] = hi
        dlo[k] = lo
        return carry

    lax.fori_loop(0, nk, tables, 0)

    lane = lax.broadcasted_iota(jnp.int32, (CHUNK, WIN), 1)

    def chunk(c, carry):
        base = pl.multiple_of(c * CHUNK, CHUNK)

        def rows_forward(b, carry):
            start = pl.multiple_of(base + b * FB, FB)
            to = pl.multiple_of(b * FB, FB)
            for w in range(nwin):
                xh = mhi[w, pl.ds(start, span), :]
                xl = mlo[w, pl.ds(start, span), :]
                x = jnp.concatenate([xh, xl, xh, jnp.zeros((256 - 3 * span, WIN), bf16)], axis=0)
                y = mm(fwd_ref[...], x)
                hi, lo = split(y)
                ahi[:, pl.ds(w * CHUNK + to, FB), :] = hi.reshape(nk, FB, WIN)
                alo[:, pl.ds(w * CHUNK + to, FB), :] = lo.reshape(nk, FB, WIN)
            return carry

        lax.fori_loop(0, CHUNK // FB, rows_forward, 0, unroll=4)
        inten[...] = jnp.zeros_like(inten)

        def cols_forward(k, carry):
            ah, al = ahi[k], alo[k]
            ch, cl = chi[k], clo[k]
            f = mm(jnp.concatenate([ah, al, ah], axis=1), jnp.concatenate([ch, ch, cl], axis=0))
            field[k] = f
            inten[...] += f * f
            return carry

        lax.fori_loop(0, nk, cols_forward, 0, unroll=8)

        t = target_ref[pl.ds(base, CHUNK), :]
        outs = []
        for w in range(nwin):
            width = min(out_win, breadth - w * out_win)
            tw = t[:, w * out_win:min(w * out_win + WIN, breadth)]
            if tw.shape[1] < WIN:
                tw = jnp.concatenate([tw, jnp.zeros((CHUNK, WIN - tw.shape[1]), f32)], axis=1)
            i = inten[w * CHUNK:(w + 1) * CHUNK, :] * inv_sum
            r = 1.0 / (1.0 + jnp.exp(-resist_slope * (i - resist_level)))
            e = (r - tw) * resist_slope * r * (1.0 - r) * (2.0 * inv_sum)
            inten[w * CHUNK:(w + 1) * CHUNK, :] = jnp.where(lane < width, e, 0.0)
            outs.append(r[:, :width])
        resist_ref[pl.ds(base, CHUNK), :] = jnp.concatenate(outs, axis=1)

        def cols_adjoint(k, carry):
            gh, gl = split(field[k] * inten[...])
            dh, dl = dhi[k], dlo[k]
            b = mm(jnp.concatenate([gh, gl, gh], axis=1), jnp.concatenate([dh, dh, dl], axis=0))
            hi, lo = split(b)
            to = pl.multiple_of(k * AB, AB)
            bhi[:, pl.ds(to, AB), :] = hi.reshape(rows3 // AB, AB, WIN)
            blo[:, pl.ds(to, AB), :] = lo.reshape(rows3 // AB, AB, WIN)
            return carry

        lax.fori_loop(0, nk, cols_adjoint, 0, unroll=8)

        def rows_adjoint(b, carry):
            start = pl.multiple_of(base + b * AB, AB)
            for w in range(nwin):
                at = w * (CHUNK // AB) + b
                p = mm(adj_ref[...], bhi[at])
                q = mm(adj_ref[:aspan, :], blo[at])
                z[w, pl.ds(start, aspan), :] += p[:aspan] + p[aspan:] + q
            return carry

        lax.fori_loop(0, CHUNK // AB, rows_adjoint, 0, unroll=4)
        return carry

    lax.fori_loop(0, height // CHUNK, chunk, 0)

    both = 2 * reach
    pieces = []
    for w in range(nwin):
        left = z[w, :, :both]
        if w:
            left = left + z[w - 1, :, out_win:]
        pieces.append(left)
        end = min(out_win, breadth + both - w * out_win)
        pieces.append(z[w, :, both:end])
    grad_ref[...] = jnp.concatenate(pieces, axis=1)


def sides(axis):
    me, count = lax.axis_index(axis), lax.axis_size(axis)
    return ((axis, me - 1, me > 0), (axis, me + 1, me < count - 1))


def greet(neighbours):
    barrier = pltpu.get_barrier_semaphore()
    for axis, at, there in neighbours:
        @pl.when(there)
        def _():
            pl.semaphore_signal(barrier, inc=1, device_id={axis: at}, device_id_type=pl.DeviceIdType.MESH)
    pl.semaphore_wait(barrier, sum(there.astype(jnp.int32) for _, _, there in neighbours))


def exchange(neighbours, sources, landing, send_sem, recv_sem):
    def copy(i):
        axis, at, _ = neighbours[i]
        return pltpu.make_async_remote_copy(
            src_ref=sources[i], dst_ref=landing.at[1 - i], send_sem=send_sem.at[i], recv_sem=recv_sem.at[1 - i],
            device_id={axis: at}, device_id_type=pl.DeviceIdType.MESH)

    def incoming(i):
        axis, at, _ = neighbours[i]
        return pltpu.make_async_remote_copy(
            src_ref=sources[i], dst_ref=landing.at[i], send_sem=send_sem.at[i], recv_sem=recv_sem.at[i],
            device_id={axis: at}, device_id_type=pl.DeviceIdType.MESH)

    for i in range(2):
        @pl.when(neighbours[i][2])
        def _():
            copy(i).start()
    for i in range(2):
        @pl.when(neighbours[i][2])
        def _():
            incoming(i).wait_recv()

        @pl.when(jnp.logical_not(neighbours[i][2]))
        def _():
            landing[i] = jnp.zeros(landing.shape[1:], f32)
    for i in range(2):
        @pl.when(neighbours[i][2])
        def _():
            copy(i).wait_send()


def pack(strip):
    width = strip.shape[1]
    folds = 128 // width
    part = strip.shape[0] // folds
    return jnp.concatenate([strip[i * part:(i + 1) * part] for i in range(folds)], axis=1)


def unpack(packed, width):
    return jnp.concatenate([packed[:, i:i + width] for i in range(0, 128, width)], axis=0)


def widen_kernel(reach, mask_ref, ext_ref, rows, colsend, cols, sems):
    height, breadth = mask_ref.shape
    up_down, left_right = sides("row"), sides("col")
    greet(up_down + left_right)
    exchange(up_down, (mask_ref.at[pl.ds(0, reach)], mask_ref.at[pl.ds(height - reach, reach)]), rows, sems.at[0], sems.at[1])
    colsend[0] = pack(jnp.concatenate([rows[0, :, :reach], mask_ref[:, :reach], rows[1, :, :reach]], axis=0))
    colsend[1] = pack(jnp.concatenate(
        [rows[0, :, breadth - reach:], mask_ref[:, breadth - reach:], rows[1, :, breadth - reach:]], axis=0))
    exchange(left_right, (colsend.at[0], colsend.at[1]), cols, sems.at[2], sems.at[3])
    left, right = unpack(cols[0], reach), unpack(cols[1], reach)
    extra = ext_ref.shape[1] - breadth - 2 * reach
    for part, lo, hi in ((rows[0], 0, reach), (mask_ref[...], reach, reach + height),
                         (rows[1], reach + height, height + 2 * reach)):
        ext_ref[lo:hi, :] = jnp.concatenate(
            [left[lo:hi], part, right[lo:hi], jnp.zeros((hi - lo, extra), f32)], axis=1)


def fold_kernel(reach, g_ref, out_ref, colsend, cols, acc, rows, sems):
    height, breadth = out_ref.shape
    up_down, left_right = sides("row"), sides("col")
    greet(up_down + left_right)
    colsend[0] = pack(g_ref[:, :reach])
    colsend[1] = pack(g_ref[:, reach + breadth:])
    exchange(left_right, (colsend.at[0], colsend.at[1]), cols, sems.at[0], sems.at[1])
    left, right = unpack(cols[0], reach), unpack(cols[1], reach)
    acc[...] = jnp.concatenate(
        [g_ref[:, reach:2 * reach] + left, g_ref[:, 2 * reach:breadth], g_ref[:, breadth:breadth + reach] + right], axis=1)
    exchange(up_down, (acc.at[pl.ds(0, reach)], acc.at[pl.ds(height + reach, reach)]), rows, sems.at[2], sems.at[3])
    out_ref[:reach, :] = acc[reach:2 * reach, :] + rows[0]
    out_ref[reach:height - reach, :] = acc[2 * reach:height, :]
    out_ref[height - reach:, :] = acc[height:height + reach, :] + rows[1]


def strips(height, breadth, reach):
    packed = pltpu.VMEM((2, (height + 2 * reach) * reach // 128, 128), f32)
    return packed, pltpu.VMEM((2, reach, breadth), f32), pltpu.SemaphoreType.DMA((4, 2))


def widen(mask, reach, need):
    height, breadth = mask.shape
    packed, rows, sems = strips(height, breadth, reach)
    vmem = pl.BlockSpec(memory_space=pltpu.VMEM)
    return pl.pallas_call(
        functools.partial(widen_kernel, reach),
        out_shape=jax.ShapeDtypeStruct((height + 2 * reach, need), f32),
        in_specs=[vmem], out_specs=vmem,
        scratch_shapes=[rows, packed, packed, sems],
        compiler_params=pltpu.CompilerParams(
            collective_id=0, has_side_effects=True, vmem_limit_bytes=16 * 1024 * 1024),
    )(mask)


def fold(grad, reach):
    height, breadth = grad.shape[0] - 2 * reach, grad.shape[1] - 2 * reach
    packed, rows, sems = strips(height, breadth, reach)
    vmem = pl.BlockSpec(memory_space=pltpu.VMEM)
    return pl.pallas_call(
        functools.partial(fold_kernel, reach),
        out_shape=jax.ShapeDtypeStruct((height, breadth), f32),
        in_specs=[vmem], out_specs=vmem,
        scratch_shapes=[packed, packed, pltpu.VMEM((height + 2 * reach, breadth), f32), rows, sems],
        compiler_params=pltpu.CompilerParams(
            collective_id=1, has_side_effects=True, vmem_limit_bytes=16 * 1024 * 1024),
    )(grad)


def toeplitz(taps, block):
    span = taps.shape[1]
    length = block + span - 1
    p = jnp.arange(span)[:, None, None]
    i = jnp.arange(block)[None, :, None]
    j = jnp.arange(length)[None, None, :]
    onehot = (j - i == p).astype(bf16)
    return jnp.einsum("kp,pij->kij", taps, onehot, preferred_element_type=f32).astype(bf16)


def shards(mask, row_taps, col_taps, kernel_weights, target, density):
    height, breadth = mask.shape
    nk, taps = row_taps.shape
    reach = (taps - 1) // 2
    count = (nk // 3) * (density[0, 0] + 1)
    active = jnp.arange(nk) < count
    inv_sum = 1.0 / jnp.sum(jnp.where(active, kernel_weights, 0.0))
    scale = jnp.where(active, jnp.sqrt(kernel_weights), 0.0)

    out_win = WIN - 2 * reach
    nwin = -(-breadth // out_win)
    need = (nwin - 1) * out_win + WIN
    ext = widen(mask, reach, need)

    rhi, rlo = split_outside(row_taps * scale[:, None])
    both = jnp.concatenate([rhi, rlo], axis=0)
    fwd = toeplitz(both, FB).reshape(2, nk * FB, FB + 2 * reach)
    fwd = jnp.concatenate([fwd[0], fwd[0], fwd[1], jnp.zeros((nk * FB, 256 - 3 * fwd.shape[2]), bf16)], axis=1)
    adj = toeplitz(both, AB).reshape(2, nk, AB, AB + 2 * reach)
    adj = adj.transpose(0, 3, 1, 2).reshape(2 * (AB + 2 * reach), nk * AB)
    avec = jnp.pad(col_taps, ((0, 0), (0, WIN - taps)))
    cvec = jnp.concatenate([col_taps[:, :1], jnp.zeros((nk, WIN - taps), f32), col_taps[:, :0:-1]], axis=1)

    eh = height + 2 * reach
    rows3 = nwin * CHUNK
    vmem = pl.BlockSpec(memory_space=pltpu.VMEM)
    resist, grad = pl.pallas_call(
        functools.partial(tile_kernel, nk, height, breadth, reach),
        out_shape=(
            jax.ShapeDtypeStruct((height, breadth), f32),
            jax.ShapeDtypeStruct((eh, breadth + 2 * reach), f32),
        ),
        in_specs=[pl.BlockSpec(memory_space=pltpu.SMEM)] + [vmem] * 6,
        out_specs=(vmem, vmem),
        scratch_shapes=[
            pltpu.VMEM((nwin, eh, WIN), bf16),
            pltpu.VMEM((nwin, eh, WIN), bf16),
            pltpu.VMEM((nk, rows3, WIN), bf16),
            pltpu.VMEM((nk, rows3, WIN), bf16),
            pltpu.VMEM((nk, rows3, WIN), f32),
            pltpu.VMEM((rows3 // AB, nk * AB, WIN), bf16),
            pltpu.VMEM((rows3 // AB, nk * AB, WIN), bf16),
            pltpu.VMEM((nwin, eh, WIN), f32),
        ] + [pltpu.VMEM((nk, WIN, WIN), bf16)] * 4 + [pltpu.VMEM((rows3, WIN), f32)],
        compiler_params=pltpu.CompilerParams(vmem_limit_bytes=60 * 1024 * 1024),
    )(inv_sum[None], ext, target, fwd, adj, cvec, avec)
    gradient = fold(grad, reach)
    return resist, gradient


def solution(mesh):
    return jax.shard_map(
        shards,
        mesh=mesh,
        in_specs=(P("row", "col"), P(), P(), P(), P("row", "col"), P("row", "col")),
        out_specs=(P("row", "col"), P("row", "col")),
        check_vma=False,
    )
```

```python
import functools

import jax
import jax.numpy as jnp
from jax import lax
from jax.experimental import pallas as pl
from jax.experimental.pallas import tpu as pltpu
from jax.sharding import PartitionSpec as P

resist_slope = 6.0
resist_level = 0.33
f32, bf16 = jnp.float32, jnp.bfloat16

FB = 16
AB = 32
CHUNK = 256
WIN = 256


def split(x):
    hi = x.astype(bf16)
    return hi, (x - hi.astype(f32)).astype(bf16)


def split_outside(x):
    hi = lax.reduce_precision(x, 8, 7)
    return hi.astype(bf16), (x - hi).astype(bf16)


def mm(a, b):
    return lax.dot_general(a, b, (((1,), (0,)), ((), ())), preferred_element_type=f32)


def tile_kernel(nk, height, breadth, reach, scal_ref, mask_ref, target_ref, fwd_ref, adj_ref, cvec_ref, avec_ref,
                resist_ref, grad_ref,
                mhi, mlo, ahi, alo, field, z, chi, clo, dhi, dlo, inten):
    out_win = WIN - 2 * reach
    nwin = -(-breadth // out_win)
    span = FB + 2 * reach
    aspan = AB + 2 * reach
    rows3 = nwin * CHUNK

    inv_sum = scal_ref[0]
    for w in range(nwin):
        m = mask_ref[:, w * out_win:w * out_win + WIN]
        hi, lo = split(m)
        mhi[w] = hi
        mlo[w] = lo
    z[...] = jnp.zeros_like(z)

    def tables(k, carry):
        row = jnp.broadcast_to(cvec_ref[pl.ds(k, 1), :], (WIN, WIN))
        hi, lo = split(pltpu.roll(row, 0, 1, stride=1, stride_axis=0))
        chi[k] = hi
        clo[k] = lo
        row = jnp.broadcast_to(avec_ref[pl.ds(k, 1), :], (WIN, WIN))
        hi, lo = split(pltpu.roll(row, 0, 1, stride=1, stride_axis=0))
        dhi[k] = hi
        dlo[k] = lo
        return carry

    lax.fori_loop(0, nk, tables, 0)

    lane = lax.broadcasted_iota(jnp.int32, (CHUNK, WIN), 1)

    def chunk(c, carry):
        base = pl.multiple_of(c * CHUNK, CHUNK)

        def rows_forward(b, carry):
            start = pl.multiple_of(base + b * FB, FB)
            to = pl.multiple_of(b * FB, FB)
            for w in range(nwin):
                xh = mhi[w, pl.ds(start, span), :]
                xl = mlo[w, pl.ds(start, span), :]
                x = jnp.concatenate([xh, xl, xh, jnp.zeros((256 - 3 * span, WIN), bf16)], axis=0)
                y = mm(fwd_ref[...], x)
                hi, lo = split(y)
                ahi[:, pl.ds(w * CHUNK + to, FB), :] = hi.reshape(nk, FB, WIN)
                alo[:, pl.ds(w * CHUNK + to, FB), :] = lo.reshape(nk, FB, WIN)
            return carry

        lax.fori_loop(0, CHUNK // FB, rows_forward, 0, unroll=4)
        inten[...] = jnp.zeros_like(inten)

        def cols_forward(k, carry):
            ah, al = ahi[k], alo[k]
            ch, cl = chi[k], clo[k]
            f = mm(jnp.concatenate([ah, al, ah], axis=1), jnp.concatenate([ch, ch, cl], axis=0))
            field[k] = f
            inten[...] += f * f
            return carry

        lax.fori_loop(0, nk, cols_forward, 0, unroll=4)

        t = target_ref[pl.ds(base, CHUNK), :]
        outs = []
        for w in range(nwin):
            width = min(out_win, breadth - w * out_win)
            tw = t[:, w * out_win:min(w * out_win + WIN, breadth)]
            if tw.shape[1] < WIN:
                tw = jnp.concatenate([tw, jnp.zeros((CHUNK, WIN - tw.shape[1]), f32)], axis=1)
            i = inten[w * CHUNK:(w + 1) * CHUNK, :] * inv_sum
            r = 1.0 / (1.0 + jnp.exp(-resist_slope * (i - resist_level)))
            e = (r - tw) * resist_slope * r * (1.0 - r) * (2.0 * inv_sum)
            inten[w * CHUNK:(w + 1) * CHUNK, :] = jnp.where(lane < width, e, 0.0)
            outs.append(r[:, :width])
        resist_ref[pl.ds(base, CHUNK), :] = jnp.concatenate(outs, axis=1)

        def cols_adjoint(k, carry):
            gh, gl = split(field[k] * inten[...])
            dh, dl = dhi[k], dlo[k]
            b = mm(jnp.concatenate([gh, gl, gh], axis=1), jnp.concatenate([dh, dh, dl], axis=0))
            hi, lo = split(b)
            ahi[k] = hi
            alo[k] = lo
            return carry

        lax.fori_loop(0, nk, cols_adjoint, 0, unroll=4)

        def rows_adjoint(b, carry):
            start = pl.multiple_of(base + b * AB, AB)
            for w in range(nwin):
                at = pl.multiple_of(w * CHUNK + b * AB, AB)
                p = mm(adj_ref[...], ahi[:, pl.ds(at, AB), :].reshape(nk * AB, WIN))
                q = mm(adj_ref[:aspan, :], alo[:, pl.ds(at, AB), :].reshape(nk * AB, WIN))
                z[w, pl.ds(start, aspan), :] += p[:aspan] + p[aspan:] + q
            return carry

        lax.fori_loop(0, CHUNK // AB, rows_adjoint, 0, unroll=4)
        return carry

    lax.fori_loop(0, height // CHUNK, chunk, 0)

    both = 2 * reach
    pieces = []
    for w in range(nwin):
        left = z[w, :, :both]
        if w:
            left = left + z[w - 1, :, out_win:]
        pieces.append(left)
        end = min(out_win, breadth + both - w * out_win)
        pieces.append(z[w, :, both:end])
    grad_ref[...] = jnp.concatenate(pieces, axis=1)


def sides(axis):
    me, count = lax.axis_index(axis), lax.axis_size(axis)
    return ((axis, me - 1, me > 0), (axis, me + 1, me < count - 1))


def greet(neighbours):
    barrier = pltpu.get_barrier_semaphore()
    for axis, at, there in neighbours:
        @pl.when(there)
        def _():
            pl.semaphore_signal(barrier, inc=1, device_id={axis: at}, device_id_type=pl.DeviceIdType.MESH)
    pl.semaphore_wait(barrier, sum(there.astype(jnp.int32) for _, _, there in neighbours))


def exchange(neighbours, sources, landing, send_sem, recv_sem):
    def copy(i):
        axis, at, _ = neighbours[i]
        return pltpu.make_async_remote_copy(
            src_ref=sources[i], dst_ref=landing.at[1 - i], send_sem=send_sem.at[i], recv_sem=recv_sem.at[1 - i],
            device_id={axis: at}, device_id_type=pl.DeviceIdType.MESH)

    def incoming(i):
        axis, at, _ = neighbours[i]
        return pltpu.make_async_remote_copy(
            src_ref=sources[i], dst_ref=landing.at[i], send_sem=send_sem.at[i], recv_sem=recv_sem.at[i],
            device_id={axis: at}, device_id_type=pl.DeviceIdType.MESH)

    for i in range(2):
        @pl.when(neighbours[i][2])
        def _():
            copy(i).start()
    for i in range(2):
        @pl.when(neighbours[i][2])
        def _():
            incoming(i).wait_recv()

        @pl.when(jnp.logical_not(neighbours[i][2]))
        def _():
            landing[i] = jnp.zeros(landing.shape[1:], f32)
    for i in range(2):
        @pl.when(neighbours[i][2])
        def _():
            copy(i).wait_send()


def pack(strip):
    width = strip.shape[1]
    folds = 128 // width
    part = strip.shape[0] // folds
    return jnp.concatenate([strip[i * part:(i + 1) * part] for i in range(folds)], axis=1)


def unpack(packed, width):
    return jnp.concatenate([packed[:, i:i + width] for i in range(0, 128, width)], axis=0)


def widen_kernel(reach, mask_ref, ext_ref, rows, colsend, cols, sems):
    height, breadth = mask_ref.shape
    up_down, left_right = sides("row"), sides("col")
    greet(up_down + left_right)
    exchange(up_down, (mask_ref.at[pl.ds(0, reach)], mask_ref.at[pl.ds(height - reach, reach)]), rows, sems.at[0], sems.at[1])
    colsend[0] = pack(jnp.concatenate([rows[0, :, :reach], mask_ref[:, :reach], rows[1, :, :reach]], axis=0))
    colsend[1] = pack(jnp.concatenate(
        [rows[0, :, breadth - reach:], mask_ref[:, breadth - reach:], rows[1, :, breadth - reach:]], axis=0))
    exchange(left_right, (colsend.at[0], colsend.at[1]), cols, sems.at[2], sems.at[3])
    left, right = unpack(cols[0], reach), unpack(cols[1], reach)
    extra = ext_ref.shape[1] - breadth - 2 * reach
    for part, lo, hi in ((rows[0], 0, reach), (mask_ref[...], reach, reach + height),
                         (rows[1], reach + height, height + 2 * reach)):
        ext_ref[lo:hi, :] = jnp.concatenate(
            [left[lo:hi], part, right[lo:hi], jnp.zeros((hi - lo, extra), f32)], axis=1)


def fold_kernel(reach, g_ref, out_ref, colsend, cols, acc, rows, sems):
    height, breadth = out_ref.shape
    up_down, left_right = sides("row"), sides("col")
    greet(up_down + left_right)
    colsend[0] = pack(g_ref[:, :reach])
    colsend[1] = pack(g_ref[:, reach + breadth:])
    exchange(left_right, (colsend.at[0], colsend.at[1]), cols, sems.at[0], sems.at[1])
    left, right = unpack(cols[0], reach), unpack(cols[1], reach)
    acc[...] = jnp.concatenate(
        [g_ref[:, reach:2 * reach] + left, g_ref[:, 2 * reach:breadth], g_ref[:, breadth:breadth + reach] + right], axis=1)
    exchange(up_down, (acc.at[pl.ds(0, reach)], acc.at[pl.ds(height + reach, reach)]), rows, sems.at[2], sems.at[3])
    out_ref[:reach, :] = acc[reach:2 * reach, :] + rows[0]
    out_ref[reach:height - reach, :] = acc[2 * reach:height, :]
    out_ref[height - reach:, :] = acc[height:height + reach, :] + rows[1]


def strips(height, breadth, reach):
    packed = pltpu.VMEM((2, (height + 2 * reach) * reach // 128, 128), f32)
    return packed, pltpu.VMEM((2, reach, breadth), f32), pltpu.SemaphoreType.DMA((4, 2))


def widen(mask, reach, need):
    height, breadth = mask.shape
    packed, rows, sems = strips(height, breadth, reach)
    vmem = pl.BlockSpec(memory_space=pltpu.VMEM)
    return pl.pallas_call(
        functools.partial(widen_kernel, reach),
        out_shape=jax.ShapeDtypeStruct((height + 2 * reach, need), f32),
        in_specs=[vmem], out_specs=vmem,
        scratch_shapes=[rows, packed, packed, sems],
        compiler_params=pltpu.CompilerParams(
            collective_id=0, has_side_effects=True, vmem_limit_bytes=16 * 1024 * 1024),
    )(mask)


def fold(grad, reach):
    height, breadth = grad.shape[0] - 2 * reach, grad.shape[1] - 2 * reach
    packed, rows, sems = strips(height, breadth, reach)
    vmem = pl.BlockSpec(memory_space=pltpu.VMEM)
    return pl.pallas_call(
        functools.partial(fold_kernel, reach),
        out_shape=jax.ShapeDtypeStruct((height, breadth), f32),
        in_specs=[vmem], out_specs=vmem,
        scratch_shapes=[packed, packed, pltpu.VMEM((height + 2 * reach, breadth), f32), rows, sems],
        compiler_params=pltpu.CompilerParams(
            collective_id=1, has_side_effects=True, vmem_limit_bytes=16 * 1024 * 1024),
    )(grad)


def toeplitz(taps, block):
    span = taps.shape[1]
    length = block + span - 1
    p = jnp.arange(span)[:, None, None]
    i = jnp.arange(block)[None, :, None]
    j = jnp.arange(length)[None, None, :]
    onehot = (j - i == p).astype(bf16)
    return jnp.einsum("kp,pij->kij", taps, onehot, preferred_element_type=f32).astype(bf16)


def shards(mask, row_taps, col_taps, kernel_weights, target, density):
    height, breadth = mask.shape
    nk, taps = row_taps.shape
    reach = (taps - 1) // 2
    count = (nk // 3) * (density[0, 0] + 1)
    active = jnp.arange(nk) < count
    inv_sum = 1.0 / jnp.sum(jnp.where(active, kernel_weights, 0.0))
    scale = jnp.where(active, jnp.sqrt(kernel_weights), 0.0)

    out_win = WIN - 2 * reach
    nwin = -(-breadth // out_win)
    need = (nwin - 1) * out_win + WIN
    ext = widen(mask, reach, need)

    rhi, rlo = split_outside(row_taps * scale[:, None])
    both = jnp.concatenate([rhi, rlo], axis=0)
    fwd = toeplitz(both, FB).reshape(2, nk * FB, FB + 2 * reach)
    fwd = jnp.concatenate([fwd[0], fwd[0], fwd[1], jnp.zeros((nk * FB, 256 - 3 * fwd.shape[2]), bf16)], axis=1)
    adj = toeplitz(both, AB).reshape(2, nk, AB, AB + 2 * reach)
    adj = adj.transpose(0, 3, 1, 2).reshape(2 * (AB + 2 * reach), nk * AB)
    avec = jnp.pad(col_taps, ((0, 0), (0, WIN - taps)))
    cvec = jnp.concatenate([col_taps[:, :1], jnp.zeros((nk, WIN - taps), f32), col_taps[:, :0:-1]], axis=1)

    eh = height + 2 * reach
    rows3 = nwin * CHUNK
    vmem = pl.BlockSpec(memory_space=pltpu.VMEM)
    resist, grad = pl.pallas_call(
        functools.partial(tile_kernel, nk, height, breadth, reach),
        out_shape=(
            jax.ShapeDtypeStruct((height, breadth), f32),
            jax.ShapeDtypeStruct((eh, breadth + 2 * reach), f32),
        ),
        in_specs=[pl.BlockSpec(memory_space=pltpu.SMEM)] + [vmem] * 6,
        out_specs=(vmem, vmem),
        scratch_shapes=[
            pltpu.VMEM((nwin, eh, WIN), bf16),
            pltpu.VMEM((nwin, eh, WIN), bf16),
            pltpu.VMEM((nk, rows3, WIN), bf16),
            pltpu.VMEM((nk, rows3, WIN), bf16),
            pltpu.VMEM((nk, rows3, WIN), f32),
            pltpu.VMEM((nwin, eh, WIN), f32),
        ] + [pltpu.VMEM((nk, WIN, WIN), bf16)] * 4 + [pltpu.VMEM((rows3, WIN), f32)],
        compiler_params=pltpu.CompilerParams(vmem_limit_bytes=63 * 1024 * 1024),
    )(inv_sum[None], ext, target, fwd, adj, cvec, avec)
    gradient = fold(grad, reach)
    return resist, gradient


def solution(mesh):
    return jax.shard_map(
        shards,
        mesh=mesh,
        in_specs=(P("row", "col"), P(), P(), P(), P("row", "col"), P("row", "col")),
        out_specs=(P("row", "col"), P("row", "col")),
        check_vma=False,
    )
```
